256 devices in a mesh: rep: 16 (over x_lo, z), fsdp: 16 (over x_hi, y, core).
Axes of the slice: x: 4 (x_hi: 2, x_lo: 2; x = x_hi * 2 + x_lo), y: 4, z: 8, core: 2. Of those that a mesh axis runs over, the one named last changes fastest.
Arguments:
- activations: bfloat16 [16, 2048, 8192], P('rep', 'fsdp'), may hold values from -6 to 6
- cotangent: bfloat16 [16, 2048, 1024], P('rep', 'fsdp'), may hold values from -0.013671875 to 0.013671875
- momentum: float32 [16, 8192, 1024], P('rep', 'fsdp'), may hold values from -6 to 6
- positions: int32 [16, 2048, 32], P('rep', 'fsdp'), may hold values from 0 to 4095, as said below
Outputs:
- new_momentum: float32 [16, 8192, 1024], P('rep', 'fsdp')
- step: float32 [8192, 1024], P('fsdp')
The draws below stay inside these ranges and needn't reach their ends.
Inputs may be any that keep to these rules, and one draw needn't show every extreme that they name: Within one replica and one group the 32 positions are distinct.
All inputs are finite; a program needn't handle non-finite values.
Results may differ from the reference program's by a relative error of at most 0.0017.
Values may be sent and summed in bfloat16 or wider, within the bound.
A program may use at most 128 MiB of HBM per device.

```python
import jax
import jax.numpy as jnp
from jax import lax

D = 8192
KVD = 1024
GROUP = 64
TOPK = 32
TOK_DEV = 128
TOK_REP = 2048
GROUPS = 2048
N_REP = 16
N_FSDP = 16


def draw_positions(key, part):

    def one_replica(subkey):
        scores = jax.random.randint(subkey, (GROUPS, GROUP * GROUP), 0, 2 ** 18) * (GROUP * GROUP)
        scores = scores + jnp.arange(GROUP * GROUP, dtype=jnp.int32)[None, :]
        return lax.top_k(scores, TOPK)[1].astype(jnp.int32)
    subkeys = jax.random.split(jax.random.fold_in(key, 71), N_REP)
    return lax.map(one_replica, subkeys)


def spiked(entries, stream_key, source, target, shards_of, factor):
    def block_of(position):
        return (jnp.arange(entries.shape[position]) // (entries.shape[position] // shards_of)).reshape((-1,) + (1,) * (entries.ndim - 1 - position))

    near = jax.random.permutation(stream_key, shards_of)[block_of(target)]
    other_side = (block_of(target) + shards_of // 2) % shards_of
    return jnp.where((block_of(source) == near) | (block_of(source) == other_side), factor * entries, entries)


def steps_of(key, shape, shards, least, top_value):
    factor_of, own = 1.0, jax.random.fold_in(key, 6)
    for axis_at, parts in shards:
        draws = jnp.exp(jax.random.uniform(jax.random.fold_in(own, axis_at), (parts,), jnp.float32, least / len(shards), top_value / len(shards)))
        factor_of = factor_of * jnp.repeat(draws, shape[axis_at] // parts).reshape([-1 if axis == axis_at else 1 for axis in range(len(shape))])
    return factor_of


def gaussian(key, shape, deviation, reach, cuts=(), kind=jnp.bfloat16):
    values = deviation * jax.random.normal(key, shape, jnp.float32)
    if cuts:
        values = values * steps_of(key, shape, cuts, -0.22, 0.18)
    return jnp.clip(values, -reach, reach).astype(kind)


def gaussian_with(own_key, dims, deviation, reach, pieces, heavy, held_as=jnp.bfloat16):
    array = deviation * jax.random.normal(own_key, dims, jnp.float32)
    if pieces:
        array = array * steps_of(own_key, dims, pieces, -0.22, 0.18)
    return jnp.clip(spiked(array, jax.random.fold_in(own_key, 3), *heavy), -reach, reach).astype(held_as)


def setup_inputs(seed: int = 0) -> dict:
    splits = jax.random.split(jax.random.key(seed), 5)
    return {
        "activations": gaussian_with(splits[0], (N_REP, TOK_REP, D), 1.0, 6.0, ((0, 16), (1, 16)), (1, 2, 16, 2.0)),
        "cotangent": gaussian(splits[1], (N_REP, TOK_REP, KVD), (100 * TOK_DEV * N_FSDP) ** -0.5, 0.013671875, ((0, 16), (1, 16))),
        "momentum": gaussian(splits[2], (N_REP, D, KVD), 1.0, 6.0, ((0, 16), (1, 16)), jnp.float32),
        "positions": draw_positions(jax.random.fold_in(splits[4], 71), 0),
    }


momentum_decay = 0.999
sharpness = 4.0

def dct_table(extent):
    frequency = jnp.arange(extent, dtype=jnp.float32)[:, None]
    location = jnp.arange(extent, dtype=jnp.float32)[None, :]
    cosines = jnp.cos(jnp.pi * (2.0 * location + 1.0) * frequency / (2.0 * extent)) * jnp.sqrt(2.0 / extent)
    return jnp.where(frequency == 0.0, cosines * jnp.sqrt(0.5), cosines)

def forward_dct(spatial, cosines):
    row_count, col_count = spatial.shape
    extent = cosines.shape[0]
    blocks = spatial.reshape(row_count // extent, extent, col_count // extent, extent)
    coeffs = jnp.einsum('hi,piqj,lj->pqhl', cosines, blocks, cosines, precision=lax.Precision.HIGHEST)
    return coeffs.reshape(-1, extent * extent)

def inverse_dct(coeffs, cosines, row_count, col_count):
    extent = cosines.shape[0]
    grid_form = coeffs.reshape(row_count // extent, col_count // extent, extent, extent)
    spatial = jnp.einsum('hi,pqhl,lj->piqj', cosines, grid_form, cosines, precision=lax.Precision.HIGHEST)
    return spatial.reshape(row_count, col_count)

def scatter_groups(values, spot_list):
    group_count = values.shape[0]
    dense_groups = jnp.zeros((group_count, GROUP * GROUP), jnp.float32)
    group_index = jnp.arange(group_count, dtype=jnp.int32)[:, None]
    return dense_groups.at[group_index, spot_list].add(values)

def reference(activations, cotangent, momentum, positions):
    cosines = dct_table(GROUP)

    def replica_step(summed, inputs):
        tokens, upstream, moment, spot_list = inputs
        tokens = tokens.reshape(N_FSDP, TOK_DEV, D)
        upstream = upstream.reshape(N_FSDP, TOK_DEV, KVD)

        def add_block(running, pair):
            product = lax.dot_general(pair[0], pair[1], (((0,), (0,)), ((), ())), preferred_element_type=jnp.float32)
            rounded = lax.optimization_barrier(product.astype(jnp.bfloat16))
            return (running + rounded.astype(jnp.float32), None)
        gradient, _ = lax.scan(add_block, jnp.zeros((D, KVD), jnp.float32), (tokens, upstream))
        updated = momentum_decay * moment + gradient
        coeffs = forward_dct(updated, cosines)
        values = jnp.take_along_axis(coeffs, spot_list, axis=1)
        own_groups = scatter_groups(values, spot_list)
        next_moment = updated - inverse_dct(own_groups, cosines, D, KVD)
        return (summed + own_groups, next_moment)
    summed, new_momentum = lax.scan(replica_step, jnp.zeros((GROUPS, GROUP * GROUP), jnp.float32), (activations, cotangent, momentum, positions))
    update = inverse_dct(summed, cosines, D, KVD)
    return (new_momentum, jnp.tanh(sharpness * update))
```

```python
import functools

import jax
import jax.numpy as jnp
import numpy as np
from jax import lax
from jax.experimental import pallas as pl
from jax.experimental.pallas import tpu as pltpu
from jax.sharding import PartitionSpec as P

GROUP = 64
MESH = pl.DeviceIdType.MESH
BF = jnp.bfloat16
F32 = jnp.float32
NEAR = ((1, 0), (3, 0), (2, 0), (1, 1), (3, 1), (2, 1), (0, 1))


def dct_table():
    k = np.arange(GROUP, dtype=np.float64)[:, None]
    n = np.arange(GROUP, dtype=np.float64)[None, :]
    table = np.cos(np.pi * (2.0 * n + 1.0) * k / (2.0 * GROUP)) * np.sqrt(2.0 / GROUP)
    table[0] *= np.sqrt(0.5)
    return table


def split_const(a):
    hi = a.astype(np.float32).astype(jnp.bfloat16)
    lo = (a - hi.astype(np.float64)).astype(np.float32).astype(jnp.bfloat16)
    return hi, lo


def tables(left, right):
    rhi, rlo = split_const(np.kron(np.eye(4), right))
    lhi, llo = split_const(np.kron(np.eye(2), left))
    return np.concatenate([rhi, rlo], 0), np.concatenate([lhi, llo, lhi], 1)


def dot(a, b):
    return jnp.dot(a, b, preferred_element_type=F32)


def split(x):
    hi = x.astype(BF)
    return hi, (x - hi.astype(F32)).astype(BF)


def right_mul(x, table_ref):
    m = x.shape[0]
    hi, lo = split(x)
    both = dot(jnp.concatenate([hi, lo], 0), table_ref[0:256, :])
    return both[:m] + both[m:] + dot(hi, table_ref[256:512, :])


def left_mul(table_ref, y):
    hi, lo = split(y)
    return dot(table_ref[...], jnp.concatenate([hi, hi, lo], 0))


def one_hots(row):
    lane = lax.broadcasted_iota(jnp.int32, (1, 128), 1)
    target = (row & 63) + (lane // 32) * 64
    wide = lax.broadcasted_iota(jnp.int32, (256, 128), 0) == target
    high = lax.broadcasted_iota(jnp.int32, (64, 128), 0) == (row >> 6)
    return wide, high


def gather_kernel(
    act, cot, mom, pos, rtab, ltab,
    upd, vall, pall,
    abuf, cbuf, xsend, xrecv, mbuf,
    c_send, c_recv, f_send, f_recv, a_send, a_recv, x_send, x_recv,
    p_send, p_recv, v_send, v_recv, local,
):
    f = lax.axis_index("fsdp")
    r = lax.axis_index("rep")
    xh, y, c = f // 8, (f // 2) % 4, f % 2
    slot = y * 2 + c

    def near(dy, dc):
        return (y + dy) % 4, (c + dc) % 2

    def fs(xx, yy, cc):
        return {"fsdp": xx * 8 + yy * 2 + cc}

    def columns(xx, s, j):
        return pl.ds(pl.multiple_of((xx * 8 + s) * 512 + j * 128, 128), 128)

    def block(s):
        return pl.ds(pl.multiple_of(s * 128, 128), 128)

    def own_copy(j):
        xx = jnp.where(j < 4, 1 - xh, xh)
        return pltpu.make_async_copy(
            act.at[:, columns(xx, slot, j % 4)], abuf.at[j, block(slot)], local.at[j]
        )

    cot_copy = pltpu.make_async_copy(cot, cbuf.at[block(slot)], local.at[8])
    mom_copy = pltpu.make_async_copy(mom, mbuf, local.at[9])
    cot_copy.start()
    for j in range(8):
        own_copy(j).start()
    mom_copy.start()

    barrier = pltpu.get_barrier_semaphore()
    for dy, dc in NEAR:
        yy, cc = near(dy, dc)
        pl.semaphore_signal(barrier, inc=1, device_id=fs(xh, yy, cc), device_id_type=MESH)
    pl.semaphore_signal(barrier, inc=1, device_id=fs(1 - xh, y, c), device_id_type=MESH)
    for d in range(1, 16):
        pl.semaphore_signal(barrier, inc=1, device_id={"rep": (r + d) % 16}, device_id_type=MESH)
    pl.semaphore_wait(barrier, 23)

    def cot_send(i, dy, dc):
        yy, cc = near(dy, dc)
        return pltpu.make_async_remote_copy(
            src_ref=cot, dst_ref=cbuf.at[block(slot)], send_sem=c_send.at[i], recv_sem=c_recv.at[i],
            device_id=fs(xh, yy, cc), device_id_type=MESH,
        )

    def cot_arrival(i, dy, dc):
        yy, cc = near(4 - dy, dc)
        s = yy * 2 + cc
        return pltpu.make_async_remote_copy(
            src_ref=cbuf.at[block(s)], dst_ref=cbuf.at[block(s)], send_sem=c_send.at[i],
            recv_sem=c_recv.at[i], device_id=fs(xh, y, 1 - c), device_id_type=MESH,
        )

    def cot_forward(i, dy):
        s = ((y + 4 - dy) % 4) * 2 + c
        return pltpu.make_async_remote_copy(
            src_ref=cbuf.at[block(s)], dst_ref=cbuf.at[block(s)], send_sem=f_send.at[i],
            recv_sem=f_recv.at[i], device_id=fs(xh, y, 1 - c), device_id_type=MESH,
        )

    def act_send(i, dy, dc, j):
        yy, cc = near(dy, dc)
        xx = jnp.where(j < 4, 1 - xh, xh)
        return pltpu.make_async_remote_copy(
            src_ref=act.at[:, columns(xx, yy * 2 + cc, j % 4)], dst_ref=abuf.at[j, block(slot)],
            send_sem=a_send.at[i, j], recv_sem=a_recv.at[i, j],
            device_id=fs(xh, yy, cc), device_id_type=MESH,
        )

    def act_arrival(i, dy, dc, j):
        yy, cc = near(4 - dy, dc)
        s = yy * 2 + cc
        return pltpu.make_async_remote_copy(
            src_ref=abuf.at[j, block(s)], dst_ref=abuf.at[j, block(s)], send_sem=a_send.at[i, j],
            recv_sem=a_recv.at[i, j], device_id=fs(xh, y, 1 - c), device_id_type=MESH,
        )

    def part_send(j):
        return pltpu.make_async_remote_copy(
            src_ref=xsend.at[block(j)], dst_ref=xrecv.at[block(j)], send_sem=x_send.at[j],
            recv_sem=x_recv.at[j], device_id=fs(1 - xh, y, c), device_id_type=MESH,
        )

    def pos_send(d, source):
        return pltpu.make_async_remote_copy(
            src_ref=pos, dst_ref=pall.at[source], send_sem=p_send.at[d - 1], recv_sem=p_recv.at[d - 1],
            device_id={"rep": (r + d) % 16}, device_id_type=MESH,
        )

    def val_send(d, j, source):
        rows = pl.ds(pl.multiple_of(j * 8, 8), 8)
        return pltpu.make_async_remote_copy(
            src_ref=vall.at[source, rows], dst_ref=vall.at[source, rows], send_sem=v_send.at[d - 1, j],
            recv_sem=v_recv.at[d - 1, j], device_id={"rep": (r + d) % 16}, device_id_type=MESH,
        )

    with_mate = NEAR[:3] + NEAR[6:]
    for i, (dy, dc) in enumerate(with_mate):
        cot_send(i, dy, dc).start()

    def send_acts(j, carry):
        for i, (dy, dc) in enumerate(NEAR):
            act_send(i, dy, dc, j).start()
        return carry

    lax.fori_loop(0, 8, send_acts, 0)
    for d in range(1, 16):
        pos_send(d, r).start()
    pall[r] = pos[...]

    for i, (dy, dc) in enumerate(with_mate):
        cot_arrival(i, dy, dc).wait_recv()
        if i < 3:
            cot_forward(i, dy).start()
    for i, (dy, dc) in enumerate(NEAR[:3]):
        s = ((y + 4 - dy) % 4) * 2 + (1 - c)
        pltpu.make_async_remote_copy(
            src_ref=cbuf.at[block(s)], dst_ref=cbuf.at[block(s)], send_sem=f_send.at[i],
            recv_sem=f_recv.at[i], device_id=fs(xh, y, 1 - c), device_id_type=MESH,
        ).wait_recv()
    cot_copy.wait()

    def product(j):
        own_copy(j).wait()
        for i, (dy, dc) in enumerate(NEAR):
            act_arrival(i, dy, dc, j).wait_recv()
        return lax.dot_general(
            abuf[j], cbuf[...], (((0,), (0,)), ((), ())), preferred_element_type=F32
        )

    def partner(j, carry):
        xsend[block(j)] = product(j).astype(BF)
        part_send(j).start()
        return carry

    lax.fori_loop(0, 4, partner, 0)
    mom_copy.wait()

    def own(j, carry):
        grad = product(j + 4)
        part_send(j).wait_recv()
        rows = block(j)
        upd[rows] = 0.999 * mbuf[rows] + (grad + xrecv[rows].astype(F32))

        def chunk(q, inner):
            cols = pl.ds(pl.multiple_of(q * 256, 256), 256)
            coeffs = left_mul(ltab, right_mul(upd[rows, cols], rtab))
            for p in range(2):
                t = j * 8 + p * 4 + q
                wide, high = one_hots(pos[pl.ds(t, 1), :])
                hi, lo = split(coeffs[p * 64 : p * 64 + 64])
                both = dot(jnp.concatenate([hi, lo], 0), wide.astype(F32).astype(BF))
                picked = jnp.where(high, both[:64] + both[64:], 0.0)
                vall[r, pl.ds(t, 1), :] = jnp.sum(picked, axis=0, keepdims=True)
            return inner

        lax.fori_loop(0, 4, chunk, 0)
        for d in range(1, 16):
            val_send(d, j, r).start()
        return carry

    lax.fori_loop(0, 4, own, 0)

    def last(j, carry):
        for d in range(1, 16):
            val_send(d, j, (r + 16 - d) % 16).wait_recv()
            val_send(d, j, r).wait_send()
        part_send(j).wait_send()
        return carry

    lax.fori_loop(0, 4, last, 0)
    for d in range(1, 16):
        pos_send(d, (r + 16 - d) % 16).wait_recv()
        pos_send(d, r).wait_send()
    for i, (dy, dc) in enumerate(with_mate):
        cot_send(i, dy, dc).wait_send()
    for i in range(3):
        cot_forward(i, NEAR[i][0]).wait_send()

    def sent(j, carry):
        for i, (dy, dc) in enumerate(NEAR):
            act_send(i, dy, dc, j).wait_send()
        return carry

    lax.fori_loop(0, 8, sent, 0)


def spread_kernel(upd, vall, pall, vown, pown, rtab, ltab, nm, st, dense):
    def masks(row, val):
        wide, high = one_hots(row)
        hi = val.astype(BF).astype(F32)
        weights = jnp.concatenate([jnp.where(high, hi, 0.0), jnp.where(high, val - hi, 0.0)], 0)
        return weights.astype(BF), wide.astype(F32).astype(BF)

    def scatter(pairs):
        w = jnp.concatenate([a for a, _ in pairs], 1)
        z = jnp.concatenate([b for _, b in pairs], 1)
        both = lax.dot_general(w, z, (((1,), (1,)), ((), ())), preferred_element_type=F32)
        return both[:64] + both[64:]

    def tile(t, carry):
        one = pl.ds(t, 1)
        cols = pl.ds(pl.multiple_of((t % 4) * 256, 256), 256)
        rows = pl.multiple_of((t // 4) * 64, 64)
        dense[pl.ds(rows, 64), cols] = scatter(
            [masks(pall[k, one, :], vall[k, one, :]) for k in range(16)]
        )
        dense[pl.ds(128 + rows, 64), cols] = scatter([masks(pown[one, :], vown[one, :])])
        return carry

    lax.fori_loop(0, 8, tile, 0)

    def chunk(q, carry):
        cols = pl.ds(pl.multiple_of(q * 256, 256), 256)
        half = right_mul(dense[:, cols], rtab)
        st[:, cols] = jnp.tanh(4.0 * left_mul(ltab, half[:128]))
        nm[:, cols] = upd[:, cols] - left_mul(ltab, half[128:])
        return carry

    lax.fori_loop(0, 4, chunk, 0)


def per_device(activations, cotangent, momentum, positions):
    b = dct_table()
    f_right, f_left = (jnp.asarray(a) for a in tables(b, b.T))
    i_right, i_left = (jnp.asarray(a) for a in tables(b.T, b))
    pos = positions.reshape(32, 128)
    vmem = pl.BlockSpec(memory_space=pltpu.VMEM)
    hbm = pl.BlockSpec(memory_space=pl.ANY)
    dma = pltpu.SemaphoreType.DMA
    upd, vall, pall = pl.pallas_call(
        gather_kernel,
        out_shape=(
            jax.ShapeDtypeStruct((512, 1024), F32),
            jax.ShapeDtypeStruct((16, 32, 128), F32),
            jax.ShapeDtypeStruct((16, 32, 128), jnp.int32),
        ),
        in_specs=[hbm, hbm, hbm, vmem, vmem, vmem],
        out_specs=(vmem, vmem, vmem),
        scratch_shapes=[
            pltpu.VMEM((8, 1024, 128), BF),
            pltpu.VMEM((1024, 1024), BF),
            pltpu.VMEM((512, 1024), BF),
            pltpu.VMEM((512, 1024), BF),
            pltpu.VMEM((512, 1024), F32),
            dma((4,)), dma((4,)), dma((3,)), dma((3,)), dma((7, 8)), dma((7, 8)), dma((4,)), dma((4,)),
            dma((15,)), dma((15,)), dma((15, 4)), dma((15, 4)), dma((10,)),
        ],
        name="gather",
        compiler_params=pltpu.CompilerParams(
            collective_id=0, has_side_effects=True, vmem_limit_bytes=40 << 20
        ),
    )(activations[0], cotangent[0], momentum[0], pos, f_right, f_left)
    me = lax.axis_index("rep")
    vown = lax.dynamic_index_in_dim(vall, me, 0, keepdims=False)
    chunk = pl.BlockSpec((128, 1024), lambda i: (i, 0))
    every = pl.BlockSpec((16, 8, 128), lambda i: (0, i, 0))
    mine = pl.BlockSpec((8, 128), lambda i: (i, 0))
    nm, st = pl.pallas_call(
        spread_kernel,
        grid=(4,),
        out_shape=(jax.ShapeDtypeStruct((512, 1024), F32), jax.ShapeDtypeStruct((512, 1024), F32)),
        in_specs=[
            chunk, every, every, mine, mine,
            pl.BlockSpec((512, 256), lambda i: (0, 0)), pl.BlockSpec((128, 384), lambda i: (0, 0)),
        ],
        out_specs=(chunk, chunk),
        scratch_shapes=[pltpu.VMEM((256, 1024), F32)],
        name="spread",
        compiler_params=pltpu.CompilerParams(vmem_limit_bytes=40 << 20),
    )(upd, vall, pall, vown, pos, i_right, i_left)
    return nm[None], st


def solution(mesh):
    return jax.shard_map(
        per_device,
        mesh=mesh,
        in_specs=(
            P("rep", "fsdp", None),
            P("rep", "fsdp", None),
            P("rep", "fsdp", None),
            P("rep", "fsdp", None),
        ),
        out_specs=(P("rep", "fsdp", None), P("fsdp", None)),
        check_vma=False,
    )
```

```python
import functools

import jax
import jax.numpy as jnp
import numpy as np
from jax import lax
from jax.experimental import pallas as pl
from jax.experimental.pallas import tpu as pltpu
from jax.sharding import PartitionSpec as P

GROUP = 64
MESH = pl.DeviceIdType.MESH
BF = jnp.bfloat16
F32 = jnp.float32
LAG = 2
NEAR = ((1, 0), (3, 0), (2, 0), (1, 1), (3, 1), (2, 1), (0, 1))


def dot(a, b):
    return jnp.dot(a, b, preferred_element_type=F32)


def split(x):
    hi = x.astype(BF)
    return hi, (x - hi.astype(F32)).astype(BF)


def right_mul(x, table_ref):
    m = x.shape[0]
    hi, lo = split(x)
    both = dot(jnp.concatenate([hi, lo], 0), table_ref[0:256, :])
    return both[:m] + both[m:] + dot(hi, table_ref[256:512, :])


def left_mul(table_ref, y):
    hi, lo = split(y)
    return dot(table_ref[...], jnp.concatenate([hi, hi, lo], 0))


def fill_tables(rt, lt):
    k = lax.broadcasted_iota(jnp.int32, (256, 256), 0)
    n = lax.broadcasted_iota(jnp.int32, (256, 256), 1)
    phase = ((2 * (n & 63) + 1) * (k & 63)) & 255
    scale = jnp.where((k & 63) == 0, 0.125, (2.0 / GROUP) ** 0.5)
    table = jnp.cos(phase.astype(F32) * (np.pi / 128)) * scale
    table = jnp.where((k >> 6) == (n >> 6), table, 0.0)
    turned = table.T
    for i, (left, right) in enumerate(((table, turned), (turned, table))):
        hi, lo = split(right)
        rt[i] = jnp.concatenate([hi, lo], 0)
        hi, lo = split(left[0:128, 0:128])
        lt[i] = jnp.concatenate([hi, lo, hi], 1)


def dot_t(a, b):
    return lax.dot_general(a, b, (((1,), (1,)), ((), ())), preferred_element_type=F32)


def t_dot(a, b):
    return lax.dot_general(a, b, (((0,), (0,)), ((), ())), preferred_element_type=F32)


def transform(x_ref, rows, rtab, ltab):
    half = [right_mul(x_ref[rows, q * 256 : q * 256 + 256], rtab) for q in range(4)]
    return [left_mul(ltab, h) for h in half]


def one_hot(iota, row):
    return jnp.where(iota == row, 1.0, 0.0).astype(BF)


def step_kernel(
    act, cot, mom, pos,
    nm, st,
    abuf, cbuf, xsend, xrecv, mbuf, pall, vall, prow, turned, orow, wide, kept, low_hot, high_hot, vrow, dense, rt, lt,
    c_send, c_recv, f_send, f_recv, a_send, a_recv, x_send, x_recv,
    p_send, p_recv, v_send, v_recv, local,
):
    f = lax.axis_index("fsdp")
    r = lax.axis_index("rep")
    xh, y, c = f // 8, (f // 2) % 4, f % 2
    slot = y * 2 + c

    def near(dy, dc):
        return (y + dy) % 4, (c + dc) % 2

    def fs(xx, yy, cc):
        return {"fsdp": xx * 8 + yy * 2 + cc}

    def block(s, n=128):
        return pl.ds(pl.multiple_of(s * n, n), n)

    def quarter(h):
        return pl.ds(h * 256, 256)

    def remote(src, dst, send, recv, device):
        return pltpu.make_async_remote_copy(
            src_ref=src, dst_ref=dst, send_sem=send, recv_sem=recv,
            device_id=device, device_id_type=MESH,
        )

    mate = fs(xh, y, 1 - c)
    over = fs(1 - xh, y, c)

    def rep(d):
        return {"rep": (r + d) % 16}

    def columns(s, j):
        xx = jnp.where(j < 4, 1 - xh, xh)
        return pl.ds(pl.multiple_of((xx * 8 + s) * 512 + (j % 4) * 128, 128), 128)

    own_act = [
        pltpu.make_async_copy(
            act.at[:, pl.ds(pl.multiple_of((xx * 8 + slot) * 512, 512), 512)],
            abuf.at[block(slot), pl.ds(k * 512, 512)], local.at[k],
        )
        for k, xx in enumerate((1 - xh, xh))
    ]
    own_cot = pltpu.make_async_copy(cot, cbuf.at[block(slot)], local.at[2])
    own_pos = pltpu.make_async_copy(pos, pall.at[block(r, 32)], local.at[3])
    get_mom = pltpu.make_async_copy(mom, mbuf, local.at[4])
    own_pos.start()

    barrier = pltpu.get_barrier_semaphore()
    for dy, dc in NEAR:
        pl.semaphore_signal(barrier, inc=1, device_id=fs(xh, *near(dy, dc)), device_id_type=MESH)
    pl.semaphore_signal(barrier, inc=1, device_id=over, device_id_type=MESH)
    for d in range(1, 16):
        pl.semaphore_signal(barrier, inc=1, device_id=rep(d), device_id_type=MESH)
    own_cot.start()
    for copy in own_act:
        copy.start()
    pl.semaphore_wait(barrier, 23)

    with_mate = tuple(enumerate(NEAR[:3] + NEAR[6:]))

    def cot_send(i, dy, dc, h):
        return remote(
            cot.at[:, quarter(h)], cbuf.at[block(slot), quarter(h)], c_send.at[i, h], c_recv.at[i, h],
            fs(xh, *near(dy, dc)),
        )

    def cot_arrival(i, dy, dc, h):
        yy, cc = near(4 - dy, dc)
        place = cbuf.at[block(yy * 2 + cc), quarter(h)]
        return remote(place, place, c_send.at[i, h], c_recv.at[i, h], mate)

    def cot_forward(i, h, cc):
        yy = (y + 4 - NEAR[i][0]) % 4
        place = cbuf.at[block(yy * 2 + cc), quarter(h)]
        return remote(place, place, f_send.at[i, h], f_recv.at[i, h], mate)

    def act_send(i, dy, dc, j):
        yy, cc = near(dy, dc)
        return remote(
            act.at[:, columns(yy * 2 + cc, j)], abuf.at[block(slot), block(j)],
            a_send.at[i, j], a_recv.at[i, j], fs(xh, yy, cc),
        )

    def act_arrival(i, dy, dc, j):
        yy, cc = near(4 - dy, dc)
        place = abuf.at[block(yy * 2 + cc), block(j)]
        return remote(place, place, a_send.at[i, j], a_recv.at[i, j], mate)

    def part_send(u, h):
        rows = block(u)
        return remote(
            xsend.at[rows, quarter(h)], xrecv.at[rows, quarter(h)], x_send.at[u, h], x_recv.at[u, h], over
        )

    def pos_send(d, source):
        return remote(
            pos, pall.at[block(source, 32)], p_send.at[d - 1], p_recv.at[d - 1], rep(d)
        )

    def val_send(d, j, source):
        place = vall.at[source, block(j, 8)]
        return remote(place, place, v_send.at[d - 1, j], v_recv.at[d - 1, j], rep(d))

    def send_acts(j, carry=0):
        for i, (dy, dc) in enumerate(NEAR):
            act_send(i, dy, dc, j).start()
        return carry

    for h in range(4):
        for i, (dy, dc) in with_mate:
            cot_send(i, dy, dc, h).start()
        send_acts(h)
        if h == 0:
            for d in range(1, 16):
                pos_send(d, r).start()
    lax.fori_loop(4, 8, send_acts, 0)
    get_mom.start()

    fill_tables(rt, lt)
    own_pos.wait()
    mine = pall[block(r, 32), :]
    turned[...] = jnp.concatenate([mine] * 4, 0).T
    lane_group = lax.broadcasted_iota(jnp.int32, (32, 128), 1) // 32
    rows32 = turned[pl.ds(0, 32, stride=4), :]
    for q in range(1, 4):
        rows32 = jnp.where(lane_group == q, turned[pl.ds(q, 32, stride=4), :], rows32)
    orow[...] = rows32
    lane1 = lax.broadcasted_iota(jnp.int32, (1, 128), 1) // 32 * 64
    iota256 = lax.broadcasted_iota(jnp.int32, (256, 128), 0)
    iota64 = lax.broadcasted_iota(jnp.int32, (64, 128), 0)

    def own_masks(p, carry):
        for q in range(4):
            t = p * 4 + q
            row = orow[pl.ds(t, 1), :]
            spread = one_hot(iota256, (row & 63) + lane1)
            wide[t] = spread
            kept[block(p, 64), q * 256 : q * 256 + 256] = dot_t(one_hot(iota64, row >> 6), spread).astype(BF)
        return carry

    lax.fori_loop(0, 8, own_masks, 0)

    def gather_rows():
        for d in range(1, 16):
            pos_send(d, (r + 16 - d) % 16).wait_recv()
        for k in range(4):
            prow[:, k * 128 : k * 128 + 128] = pall[k * 128 : k * 128 + 128, :].T

    iota512 = lax.broadcasted_iota(jnp.int32, (64, 512), 0).astype(jnp.int16)

    def all_masks(h):
        def group(g, carry):
            row = prow[pl.ds(g, 1), :]
            for part, out in ((row & 63, low_hot), (row >> 6, high_hot)):
                part = jnp.broadcast_to(part.astype(jnp.int16), (64, 512))
                out[g] = jnp.where(iota512 == part, jnp.ones((), BF), jnp.zeros((), BF))
            return carry

        lax.fori_loop(h * 32, h * 32 + 32, group, 0)

    def wait_acts(j):
        for i, (dy, dc) in enumerate(NEAR):
            act_arrival(i, dy, dc, j).wait_recv()

    for h in range(4):
        for i, (dy, dc) in with_mate:
            cot_arrival(i, dy, dc, h).wait_recv()
            if i < 3:
                cot_forward(i, h, c).start()
        for i in range(3):
            cot_forward(i, h, 1 - c).wait_recv()
        if h == 0:
            own_cot.wait()
            own_act[0].wait()
        else:
            done = 128 * h
            xsend[0:done, quarter(h)] = t_dot(abuf[:, 0:done], cbuf[:, quarter(h)]).astype(BF)
            for u in range(h):
                part_send(u, h).start()
        wait_acts(h)
        upto = 256 * (h + 1)
        xsend[block(h), 0:upto] = t_dot(abuf[:, block(h)], cbuf[:, 0:upto]).astype(BF)
        for k in range(h + 1):
            part_send(h, k).start()
        if h == 0:
            gather_rows()
        all_masks(h)

    get_mom.wait()
    own_act[1].wait()

    def momentum(j):
        rows = block(j)
        wait_acts(j + 4)
        grad = t_dot(abuf[:, block(j + 4)], cbuf[...])
        for h in range(4):
            part_send(j, h).wait_recv()
        nm[rows, :] = 0.999 * mbuf[rows, :] + (grad + xrecv[rows, :].astype(F32))
        coeffs = transform(nm, rows, rt.at[0], lt.at[0])
        for q in range(4):
            cols = pl.ds(q * 256, 256)
            dense[:, cols] = coeffs[q] * kept[rows, cols].astype(F32)
            for p in range(2):
                t = j * 8 + p * 4 + q
                hi, lo = split(coeffs[q][p * 64 : p * 64 + 64])
                both = dot(jnp.concatenate([hi, lo], 0), wide[t])
                high = iota64 == (orow[pl.ds(t, 1), :] >> 6)
                picked = jnp.where(high, both[:64] + both[64:], 0.0)
                vall[r, pl.ds(t, 1), :] = jnp.sum(picked, axis=0, keepdims=True)
        for d in range(1, 16):
            val_send(d, j, r).start()
        for q, own in enumerate(transform(dense, pl.ds(0, 128), rt.at[1], lt.at[1])):
            cols = pl.ds(q * 256, 256)
            nm[rows, cols] = nm[rows, cols] - own

    lane8 = lax.broadcasted_iota(jnp.int32, (8, 128), 1) // 32

    def update(j):
        for d in range(1, 16):
            val_send(d, j, (r + 16 - d) % 16).wait_recv()
        for k in range(4):
            tiles = [vall[4 * k + b, block(j, 8), :] for b in range(4)]
            for q in range(4):
                merged = None
                for b in range(4):
                    shift = (b - q) * 32 % 128
                    moved = pltpu.roll(tiles[b], shift, 1) if shift else tiles[b]
                    merged = moved if b == 0 else jnp.where(lane8 == b, moved, merged)
                vrow[q, :, k * 128 : k * 128 + 128] = merged
        for t in range(8):
            parts = []
            for q in range(4):
                g = (j * 8 + t) * 4 + q
                val = vrow[q, t : t + 1, :]
                hi = val.astype(BF)
                lo = (val - hi.astype(F32)).astype(BF)
                hot = high_hot[g]
                both = dot_t(jnp.concatenate([hot * hi, hot * lo], 0), low_hot[g])
                parts.append(both[:64] + both[64:])
            row, col = t // 4 * 64, t % 4 * 256
            dense[row : row + 64, col : col + 256] = jnp.concatenate(parts, 1)
        for q, out in enumerate(transform(dense, pl.ds(0, 128), rt.at[1], lt.at[1])):
            st[block(j), q * 256 : q * 256 + 256] = jnp.tanh(4.0 * out)

    def stage(j, carry):
        @pl.when(j < 4)
        def _():
            momentum(j)

        @pl.when(j >= LAG)
        def _():
            update(j - LAG)

        return carry

    lax.fori_loop(0, 4 + LAG, stage, 0)

    for h in range(4):
        for i, (dy, dc) in with_mate:
            cot_send(i, dy, dc, h).wait_send()
        for i in range(3):
            cot_forward(i, h, c).wait_send()
        for u in range(4):
            part_send(u, h).wait_send()
    for d in range(1, 16):
        pos_send(d, r).wait_send()

    def sent(j, carry):
        for i, (dy, dc) in enumerate(NEAR):
            act_send(i, dy, dc, j).wait_send()
            act_send(i, dy, dc, j + 4).wait_send()
        for d in range(1, 16):
            val_send(d, j, r).wait_send()
        return carry

    lax.fori_loop(0, 4, sent, 0)


def store_kernel(a, b, a_out, b_out, sems):
    copies = [pltpu.make_async_copy(a, a_out, sems.at[0]), pltpu.make_async_copy(b, b_out, sems.at[1])]
    for copy in copies:
        copy.start()
    for copy in copies:
        copy.wait()


def per_device(activations, cotangent, momentum, positions):
    vmem = pl.BlockSpec(memory_space=pltpu.VMEM)
    hbm = pl.BlockSpec(memory_space=pltpu.HBM)
    dma = pltpu.SemaphoreType.DMA
    rows = jax.ShapeDtypeStruct((512, 1024), F32)
    nm, st = pl.pallas_call(
        step_kernel,
        out_shape=(rows, rows),
        in_specs=[hbm] * 4,
        out_specs=(vmem, vmem),
        scratch_shapes=[
            pltpu.VMEM((1024, 1024), BF),
            pltpu.VMEM((1024, 1024), BF),
            pltpu.VMEM((512, 1024), BF),
            pltpu.VMEM((512, 1024), BF),
            pltpu.VMEM((512, 1024), F32),
            pltpu.VMEM((512, 128), jnp.int32),
            pltpu.VMEM((16, 32, 128), F32),
            pltpu.VMEM((128, 512), jnp.int32),
            pltpu.VMEM((128, 128), jnp.int32),
            pltpu.VMEM((32, 128), jnp.int32),
            pltpu.VMEM((32, 256, 128), BF),
            pltpu.VMEM((512, 1024), BF),
            pltpu.VMEM((128, 64, 512), BF),
            pltpu.VMEM((128, 64, 512), BF),
            pltpu.VMEM((4, 8, 512), F32),
            pltpu.VMEM((128, 1024), F32),
            pltpu.VMEM((2, 512, 256), BF),
            pltpu.VMEM((2, 128, 384), BF),
            dma((4, 4)), dma((4, 4)), dma((3, 4)), dma((3, 4)), dma((7, 8)), dma((7, 8)), dma((4, 4)), dma((4, 4)),
            dma((15,)), dma((15,)), dma((15, 4)), dma((15, 4)), dma((5,)),
        ],
        name="step",
        compiler_params=pltpu.CompilerParams(
            collective_id=0, has_side_effects=True, vmem_limit_bytes=48 << 20
        ),
    )(activations[0], cotangent[0], momentum[0], positions[0].T)
    nm, st = pl.pallas_call(
        store_kernel,
        out_shape=(rows, rows),
        in_specs=[vmem, vmem],
        out_specs=(hbm, hbm),
        scratch_shapes=[dma((2,))],
        name="store",
        compiler_params=pltpu.CompilerParams(vmem_limit_bytes=1 << 20),
    )(nm, st)
    return nm[None], st


def solution(mesh):
    return jax.shard_map(
        per_device,
        mesh=mesh,
        in_specs=(
            P("rep", "fsdp", None),
            P("rep", "fsdp", None),
            P("rep", "fsdp", None),
            P("rep", "fsdp", None),
        ),
        out_specs=(P("rep", "fsdp", None), P("fsdp", None)),
        check_vma=False,
    )
```

```python
import functools

import jax
import jax.numpy as jnp
import numpy as np
from jax import lax
from jax.experimental import pallas as pl
from jax.experimental.pallas import tpu as pltpu
from jax.sharding import PartitionSpec as P

GROUP = 64
MESH = pl.DeviceIdType.MESH
BF = jnp.bfloat16
F32 = jnp.float32
LAG = 2
NEAR = ((2, 0), (1, 0), (3, 0), (2, 1), (1, 1), (3, 1), (0, 1))
FAR_FIRST = (12, 4, 11, 13, 3, 5, 10, 14, 2, 6, 9, 15, 1, 7, 8)


def dot(a, b):
    return jnp.dot(a, b, preferred_element_type=F32)


def split(x):
    hi = x.astype(BF)
    return hi, (x - hi.astype(F32)).astype(BF)


def right_mul(x, table_ref):
    m = x.shape[0]
    hi, lo = split(x)
    both = dot(jnp.concatenate([hi, lo], 0), table_ref[0:256, :])
    return both[:m] + both[m:] + dot(hi, table_ref[256:512, :])


def left_mul(table_ref, y):
    hi, lo = split(y)
    return dot(table_ref[...], jnp.concatenate([hi, hi, lo], 0))


def fill_tables(rt, lt):
    k = lax.broadcasted_iota(jnp.int32, (256, 256), 0)
    n = lax.broadcasted_iota(jnp.int32, (256, 256), 1)
    phase = ((2 * (n & 63) + 1) * (k & 63)) & 255
    scale = jnp.where((k & 63) == 0, 0.125, (2.0 / GROUP) ** 0.5)
    table = jnp.cos(phase.astype(F32) * (np.pi / 128)) * scale
    table = jnp.where((k >> 6) == (n >> 6), table, 0.0)
    turned = table.T
    for i, (left, right) in enumerate(((table, turned), (turned, table))):
        hi, lo = split(right)
        rt[i] = jnp.concatenate([hi, lo], 0)
        hi, lo = split(left[0:128, 0:128])
        lt[i] = jnp.concatenate([hi, lo, hi], 1)


def dot_t(a, b):
    return lax.dot_general(a, b, (((1,), (1,)), ((), ())), preferred_element_type=F32)


def t_dot(a, b):
    return lax.dot_general(a, b, (((0,), (0,)), ((), ())), preferred_element_type=F32)


def transform(x_ref, rows, rtab, ltab):
    half = [right_mul(x_ref[rows, q * 256 : q * 256 + 256], rtab) for q in range(4)]
    return [left_mul(ltab, h) for h in half]


def one_hot(iota, row):
    return jnp.where(iota == row, 1.0, 0.0).astype(BF)


def step_kernel(
    act, cot, mom, pos,
    nm, st,
    abuf, cbuf, xsend, xrecv, mbuf, pall, vall, prow, turned, orow, wide, kept, low_hot, high_hot, vrow, dense, rt, lt,
    c_send, c_recv, f_send, f_recv, a_send, a_recv, x_send, x_recv,
    p_send, p_recv, v_send, v_recv, local,
):
    f = lax.axis_index("fsdp")
    r = lax.axis_index("rep")
    xh, y, c = f // 8, (f // 2) % 4, f % 2
    slot = y * 2 + c

    def near(dy, dc):
        return (y + dy) % 4, (c + dc) % 2

    def fs(xx, yy, cc):
        return {"fsdp": xx * 8 + yy * 2 + cc}

    def block(s, n=128):
        return pl.ds(pl.multiple_of(s * n, n), n)

    def quarter(h):
        return pl.ds(h * 256, 256)

    def remote(src, dst, send, recv, device):
        return pltpu.make_async_remote_copy(
            src_ref=src, dst_ref=dst, send_sem=send, recv_sem=recv,
            device_id=device, device_id_type=MESH,
        )

    mate = fs(xh, y, 1 - c)
    over = fs(1 - xh, y, c)

    def rep(d):
        return {"rep": (r + d) % 16}

    def columns(s, j):
        xx = jnp.where(j < 4, 1 - xh, xh)
        return pl.ds(pl.multiple_of((xx * 8 + s) * 512 + (j % 4) * 128, 128), 128)

    own_act = [
        pltpu.make_async_copy(
            act.at[:, pl.ds(pl.multiple_of((xx * 8 + slot) * 512, 512), 512)],
            abuf.at[block(slot), pl.ds(k * 512, 512)], local.at[k],
        )
        for k, xx in enumerate((1 - xh, xh))
    ]
    own_cot = pltpu.make_async_copy(cot, cbuf.at[block(slot)], local.at[2])
    own_pos = pltpu.make_async_copy(pos, pall.at[block(r, 32)], local.at[3])
    get_mom = pltpu.make_async_copy(mom, mbuf, local.at[4])
    own_pos.start()

    barrier = pltpu.get_barrier_semaphore()
    for dy, dc in NEAR:
        pl.semaphore_signal(barrier, inc=1, device_id=fs(xh, *near(dy, dc)), device_id_type=MESH)
    pl.semaphore_signal(barrier, inc=1, device_id=over, device_id_type=MESH)
    for d in range(1, 16):
        pl.semaphore_signal(barrier, inc=1, device_id=rep(d), device_id_type=MESH)
    own_cot.start()
    for copy in own_act:
        copy.start()
    pl.semaphore_wait(barrier, 23)

    with_mate = tuple(enumerate(NEAR[:3] + NEAR[6:]))

    def cot_send(i, dy, dc, h):
        return remote(
            cot.at[:, quarter(h)], cbuf.at[block(slot), quarter(h)], c_send.at[i, h], c_recv.at[i, h],
            fs(xh, *near(dy, dc)),
        )

    def cot_arrival(i, dy, dc, h):
        yy, cc = near(4 - dy, dc)
        place = cbuf.at[block(yy * 2 + cc), quarter(h)]
        return remote(place, place, c_send.at[i, h], c_recv.at[i, h], mate)

    def cot_forward(i, h, cc):
        yy = (y + 4 - NEAR[i][0]) % 4
        place = cbuf.at[block(yy * 2 + cc), quarter(h)]
        return remote(place, place, f_send.at[i, h], f_recv.at[i, h], mate)

    def act_send(i, dy, dc, j):
        yy, cc = near(dy, dc)
        return remote(
            act.at[:, columns(yy * 2 + cc, j)], abuf.at[block(slot), block(j)],
            a_send.at[i, j], a_recv.at[i, j], fs(xh, yy, cc),
        )

    def act_arrival(i, dy, dc, j):
        yy, cc = near(4 - dy, dc)
        place = abuf.at[block(yy * 2 + cc), block(j)]
        return remote(place, place, a_send.at[i, j], a_recv.at[i, j], mate)

    def part_send(u, h):
        rows = block(u)
        return remote(
            xsend.at[rows, quarter(h)], xrecv.at[rows, quarter(h)], x_send.at[u, h], x_recv.at[u, h], over
        )

    def pos_send(d, source):
        return remote(
            pos, pall.at[block(source, 32)], p_send.at[d - 1], p_recv.at[d - 1], rep(d)
        )

    def val_send(d, j, source):
        place = vall.at[source, block(j, 8)]
        return remote(place, place, v_send.at[d - 1, j], v_recv.at[d - 1, j], rep(d))

    def send_acts(j, carry=0):
        for i, (dy, dc) in enumerate(NEAR):
            act_send(i, dy, dc, j).start()
        return carry

    for h in range(4):
        for i, (dy, dc) in with_mate:
            cot_send(i, dy, dc, h).start()
        if h == 3:
            send_acts(4)
        send_acts(h)
        if h == 0:
            for d in range(1, 16):
                pos_send(d, r).start()
    lax.fori_loop(5, 8, send_acts, 0)
    get_mom.start()

    own_pos.wait()
    mine = pall[block(r, 32), :]
    turned[...] = jnp.concatenate([mine] * 4, 0).T
    lane_group = lax.broadcasted_iota(jnp.int32, (32, 128), 1) // 32
    rows32 = turned[pl.ds(0, 32, stride=4), :]
    for q in range(1, 4):
        rows32 = jnp.where(lane_group == q, turned[pl.ds(q, 32, stride=4), :], rows32)
    orow[...] = rows32
    lane1 = lax.broadcasted_iota(jnp.int32, (1, 128), 1) // 32 * 64
    iota256 = lax.broadcasted_iota(jnp.int32, (256, 128), 0)
    iota64 = lax.broadcasted_iota(jnp.int32, (64, 128), 0)

    def own_masks(p, carry):
        for q in range(4):
            t = p * 4 + q
            row = orow[pl.ds(t, 1), :]
            spread = one_hot(iota256, (row & 63) + lane1)
            wide[t] = spread
            kept[block(p, 64), q * 256 : q * 256 + 256] = dot_t(one_hot(iota64, row >> 6), spread).astype(BF)
        return carry

    def gather_rows():
        for d in range(1, 16):
            pos_send(d, (r + 16 - d) % 16).wait_recv()
        for k in range(4):
            prow[:, k * 128 : k * 128 + 128] = pall[k * 128 : k * 128 + 128, :].T

    iota512 = lax.broadcasted_iota(jnp.int32, (64, 512), 0).astype(jnp.int16)

    def all_masks(first):
        def group(g, carry):
            row = prow[pl.ds(g, 1), :]
            for part, out in ((row & 63, low_hot), (row >> 6, high_hot)):
                part = jnp.broadcast_to(part.astype(jnp.int16), (64, 512))
                out[g] = jnp.where(iota512 == part, jnp.ones((), BF), jnp.zeros((), BF))
            return carry

        lax.fori_loop(first, first + 64, group, 0)

    def wait_acts(j):
        for i, (dy, dc) in enumerate(NEAR):
            act_arrival(i, dy, dc, j).wait_recv()

    for h in range(4):
        for i, (dy, dc) in with_mate:
            cot_arrival(i, dy, dc, h).wait_recv()
            if i < 3:
                cot_forward(i, h, c).start()
        for i in range(3):
            cot_forward(i, h, 1 - c).wait_recv()
        if h == 0:
            own_cot.wait()
            own_act[0].wait()
        else:
            done = 128 * h
            xsend[0:done, quarter(h)] = t_dot(abuf[:, 0:done], cbuf[:, quarter(h)]).astype(BF)
            for u in range(h):
                part_send(u, h).start()
        wait_acts(h)
        upto = 256 * (h + 1)
        xsend[block(h), 0:upto] = t_dot(abuf[:, block(h)], cbuf[:, 0:upto]).astype(BF)
        for k in range(h + 1):
            part_send(h, k).start()
        if h == 0:
            fill_tables(rt, lt)
            lax.fori_loop(0, 8, own_masks, 0)
        elif h == 1:
            gather_rows()
            all_masks(0)
        elif h == 2:
            all_masks(64)

    get_mom.wait()
    own_act[1].wait()

    def momentum(j):
        rows = block(j)
        wait_acts(j + 4)
        grad = t_dot(abuf[:, block(j + 4)], cbuf[...])
        for h in range(4):
            part_send(j, h).wait_recv()
        nm[rows, :] = 0.999 * mbuf[rows, :] + (grad + xrecv[rows, :].astype(F32))
        coeffs = transform(nm, rows, rt.at[0], lt.at[0])
        for q in range(4):
            cols = pl.ds(q * 256, 256)
            dense[:, cols] = coeffs[q] * kept[rows, cols].astype(F32)
            for p in range(2):
                t = j * 8 + p * 4 + q
                hi, lo = split(coeffs[q][p * 64 : p * 64 + 64])
                both = dot(jnp.concatenate([hi, lo], 0), wide[t])
                high = iota64 == (orow[pl.ds(t, 1), :] >> 6)
                picked = jnp.where(high, both[:64] + both[64:], 0.0)
                vall[r, pl.ds(t, 1), :] = jnp.sum(picked, axis=0, keepdims=True)
        for d in FAR_FIRST:
            val_send(d, j, r).start()
        for q, own in enumerate(transform(dense, pl.ds(0, 128), rt.at[1], lt.at[1])):
            cols = pl.ds(q * 256, 256)
            nm[rows, cols] = nm[rows, cols] - own

    lane8 = lax.broadcasted_iota(jnp.int32, (8, 128), 1) // 32

    def update(j):
        for d in range(1, 16):
            val_send(d, j, (r + 16 - d) % 16).wait_recv()
        for k in range(4):
            tiles = [vall[4 * k + b, block(j, 8), :] for b in range(4)]
            for q in range(4):
                merged = None
                for b in range(4):
                    shift = (b - q) * 32 % 128
                    moved = pltpu.roll(tiles[b], shift, 1) if shift else tiles[b]
                    merged = moved if b == 0 else jnp.where(lane8 == b, moved, merged)
                vrow[q, :, k * 128 : k * 128 + 128] = merged
        for t in range(8):
            parts = []
            for q in range(4):
                g = (j * 8 + t) * 4 + q
                val = vrow[q, t : t + 1, :]
                hi = val.astype(BF)
                lo = (val - hi.astype(F32)).astype(BF)
                hot = high_hot[g]
                both = dot_t(jnp.concatenate([hot * hi, hot * lo], 0), low_hot[g])
                parts.append(both[:64] + both[64:])
            row, col = t // 4 * 64, t % 4 * 256
            dense[row : row + 64, col : col + 256] = jnp.concatenate(parts, 1)
        for q, out in enumerate(transform(dense, pl.ds(0, 128), rt.at[1], lt.at[1])):
            st[block(j), q * 256 : q * 256 + 256] = jnp.tanh(4.0 * out)

    def all_sent():
        for h in range(4):
            for i, (dy, dc) in with_mate:
                cot_send(i, dy, dc, h).wait_send()
            for i in range(3):
                cot_forward(i, h, c).wait_send()
        for d in range(1, 16):
            pos_send(d, r).wait_send()

        def sent(j, carry):
            for i, (dy, dc) in enumerate(NEAR):
                act_send(i, dy, dc, j).wait_send()
                act_send(i, dy, dc, j + 4).wait_send()
            for h in range(4):
                part_send(j, h).wait_send()
            return carry

        lax.fori_loop(0, 4, sent, 0)

        def values_sent(j, carry):
            for d in range(1, 16):
                val_send(d, j, r).wait_send()
            return carry

        lax.fori_loop(0, 3, values_sent, 0)

    def stage(j, carry):
        @pl.when(j < 4)
        def _():
            momentum(j)

        @pl.when(j >= LAG)
        def _():
            update(j - LAG)

        @pl.when(j == 4)
        def _():
            all_sent()

        return carry

    lax.fori_loop(0, 4 + LAG, stage, 0)

    for d in range(1, 16):
        val_send(d, 3, r).wait_send()


def store_kernel(a, b, a_out, b_out, sems):
    copies = [
        pltpu.make_async_copy(src.at[pl.ds(k * 128, 128)], dst.at[pl.ds(k * 128, 128)], sems.at[i, k])
        for i, (src, dst) in enumerate(((a, a_out), (b, b_out)))
        for k in range(4)
    ]
    for copy in copies:
        copy.start()
    for copy in copies:
        copy.wait()


def per_device(activations, cotangent, momentum, positions):
    vmem = pl.BlockSpec(memory_space=pltpu.VMEM)
    hbm = pl.BlockSpec(memory_space=pltpu.HBM)
    dma = pltpu.SemaphoreType.DMA
    rows = jax.ShapeDtypeStruct((512, 1024), F32)
    nm, st = pl.pallas_call(
        step_kernel,
        out_shape=(rows, rows),
        in_specs=[hbm] * 4,
        out_specs=(vmem, vmem),
        scratch_shapes=[
            pltpu.VMEM((1024, 1024), BF),
            pltpu.VMEM((1024, 1024), BF),
            pltpu.VMEM((512, 1024), BF),
            pltpu.VMEM((512, 1024), BF),
            pltpu.VMEM((512, 1024), F32),
            pltpu.VMEM((512, 128), jnp.int32),
            pltpu.VMEM((16, 32, 128), F32),
            pltpu.VMEM((128, 512), jnp.int32),
            pltpu.VMEM((128, 128), jnp.int32),
            pltpu.VMEM((32, 128), jnp.int32),
            pltpu.VMEM((32, 256, 128), BF),
            pltpu.VMEM((512, 1024), BF),
            pltpu.VMEM((128, 64, 512), BF),
            pltpu.VMEM((128, 64, 512), BF),
            pltpu.VMEM((4, 8, 512), F32),
            pltpu.VMEM((128, 1024), F32),
            pltpu.VMEM((2, 512, 256), BF),
            pltpu.VMEM((2, 128, 384), BF),
            dma((4, 4)), dma((4, 4)), dma((3, 4)), dma((3, 4)), dma((7, 8)), dma((7, 8)), dma((4, 4)), dma((4, 4)),
            dma((15,)), dma((15,)), dma((15, 4)), dma((15, 4)), dma((5,)),
        ],
        name="step",
        compiler_params=pltpu.CompilerParams(
            collective_id=0, has_side_effects=True, vmem_limit_bytes=48 << 20
        ),
    )(activations[0], cotangent[0], momentum[0], positions[0].T)
    nm, st = pl.pallas_call(
        store_kernel,
        out_shape=(rows, rows),
        in_specs=[vmem, vmem],
        out_specs=(hbm, hbm),
        scratch_shapes=[dma((2, 4))],
        name="store",
        compiler_params=pltpu.CompilerParams(vmem_limit_bytes=1 << 20),
    )(nm, st)
    return nm[None], st


def solution(mesh):
    return jax.shard_map(
        per_device,
        mesh=mesh,
        in_specs=(
            P("rep", "fsdp", None),
            P("rep", "fsdp", None),
            P("rep", "fsdp", None),
            P("rep", "fsdp", None),
        ),
        out_specs=(P("rep", "fsdp", None), P("fsdp", None)),
        check_vma=False,
    )
```

```python
import functools

import jax
import jax.numpy as jnp
import numpy as np
from jax import lax
from jax.experimental import pallas as pl
from jax.experimental.pallas import tpu as pltpu
from jax.sharding import PartitionSpec as P

GROUP = 64
MESH = pl.DeviceIdType.MESH
BF = jnp.bfloat16
F32 = jnp.float32
LAG = 2
NEAR = ((2, 0), (1, 0), (3, 0), (2, 1), (1, 1), (3, 1), (0, 1))
FAR_FIRST = (12, 4, 11, 13, 3, 5, 10, 14, 2, 6, 9, 15, 1, 7, 8)


def dot(a, b):
    return jnp.dot(a, b, preferred_element_type=F32)


def split(x):
    hi = x.astype(BF)
    return hi, (x - hi.astype(F32)).astype(BF)


def right_mul(x, table_ref):
    m = x.shape[0]
    hi, lo = split(x)
    both = dot(jnp.concatenate([hi, lo], 0), table_ref[0:256, :])
    return both[:m] + both[m:] + dot(hi, table_ref[256:512, :])


def left_mul(table_ref, y):
    hi, lo = split(y)
    return dot(table_ref[...], jnp.concatenate([hi, hi, lo], 0))


def fill_tables(rt, lt):
    k = lax.broadcasted_iota(jnp.int32, (256, 256), 0)
    n = lax.broadcasted_iota(jnp.int32, (256, 256), 1)
    phase = ((2 * (n & 63) + 1) * (k & 63)) & 255
    scale = jnp.where((k & 63) == 0, 0.125, (2.0 / GROUP) ** 0.5)
    table = jnp.cos(phase.astype(F32) * (np.pi / 128)) * scale
    table = jnp.where((k >> 6) == (n >> 6), table, 0.0)
    turned = table.T
    for i, (left, right) in enumerate(((table, turned), (turned, table))):
        hi, lo = split(right)
        rt[i] = jnp.concatenate([hi, lo], 0)
        hi, lo = split(left[0:128, 0:128])
        lt[i] = jnp.concatenate([hi, lo, hi], 1)


def dot_t(a, b):
    return lax.dot_general(a, b, (((1,), (1,)), ((), ())), preferred_element_type=F32)


def t_dot(a, b):
    return lax.dot_general(a, b, (((0,), (0,)), ((), ())), preferred_element_type=F32)


def transform(x_ref, rows, rtab, ltab):
    half = [right_mul(x_ref[rows, q * 256 : q * 256 + 256], rtab) for q in range(4)]
    return [left_mul(ltab, h) for h in half]


def one_hot(iota, row):
    return jnp.where(iota == row, 1.0, 0.0).astype(BF)


def step_kernel(
    act, cot, mom, pos,
    nm, st,
    abuf, cbuf, xsend, xrecv, mbuf, pall, vall, prow, turned, orow, wide, kept, low_hot, high_hot, vrow, dense, rt, lt,
    c_send, c_recv, f_send, f_recv, a_send, a_recv, x_send, x_recv,
    p_send, p_recv, v_send, v_recv, local,
):
    f = lax.axis_index("fsdp")
    r = lax.axis_index("rep")
    xh, y, c = f // 8, (f // 2) % 4, f % 2
    slot = y * 2 + c

    def near(dy, dc):
        return (y + dy) % 4, (c + dc) % 2

    def fs(xx, yy, cc):
        return {"fsdp": xx * 8 + yy * 2 + cc}

    def block(s, n=128):
        return pl.ds(pl.multiple_of(s * n, n), n)

    def quarter(h):
        return pl.ds(h * 256, 256)

    def remote(src, dst, send, recv, device):
        return pltpu.make_async_remote_copy(
            src_ref=src, dst_ref=dst, send_sem=send, recv_sem=recv,
            device_id=device, device_id_type=MESH,
        )

    mate = fs(xh, y, 1 - c)
    over = fs(1 - xh, y, c)

    def rep(d):
        return {"rep": (r + d) % 16}

    def columns(s, j):
        xx = jnp.where(j < 4, 1 - xh, xh)
        return pl.ds(pl.multiple_of((xx * 8 + s) * 512 + (j % 4) * 128, 128), 128)

    own_act = [
        pltpu.make_async_copy(
            act.at[:, pl.ds(pl.multiple_of((xx * 8 + slot) * 512, 512), 512)],
            abuf.at[block(slot), pl.ds(k * 512, 512)], local.at[k],
        )
        for k, xx in enumerate((1 - xh, xh))
    ]
    own_cot = pltpu.make_async_copy(cot, cbuf.at[block(slot)], local.at[2])
    own_pos = pltpu.make_async_copy(pos, pall.at[block(r, 32)], local.at[3])
    get_mom = pltpu.make_async_copy(mom, mbuf, local.at[4])
    own_pos.start()

    barrier = pltpu.get_barrier_semaphore()
    for dy, dc in NEAR:
        pl.semaphore_signal(barrier, inc=1, device_id=fs(xh, *near(dy, dc)), device_id_type=MESH)
    pl.semaphore_signal(barrier, inc=1, device_id=over, device_id_type=MESH)
    for d in range(1, 16):
        pl.semaphore_signal(barrier, inc=1, device_id=rep(d), device_id_type=MESH)
    own_cot.start()
    for copy in own_act:
        copy.start()
    pl.semaphore_wait(barrier, 23)

    with_mate = tuple(enumerate(NEAR[:3] + NEAR[6:]))

    def cot_send(i, dy, dc, h):
        return remote(
            cot.at[:, quarter(h)], cbuf.at[block(slot), quarter(h)], c_send.at[i, h], c_recv.at[i, h],
            fs(xh, *near(dy, dc)),
        )

    def cot_arrival(i, dy, dc, h):
        yy, cc = near(4 - dy, dc)
        place = cbuf.at[block(yy * 2 + cc), quarter(h)]
        return remote(place, place, c_send.at[i, h], c_recv.at[i, h], mate)

    def cot_forward(i, h, cc):
        yy = (y + 4 - NEAR[i][0]) % 4
        place = cbuf.at[block(yy * 2 + cc), quarter(h)]
        return remote(place, place, f_send.at[i, h], f_recv.at[i, h], mate)

    def act_send(i, dy, dc, j):
        yy, cc = near(dy, dc)
        return remote(
            act.at[:, columns(yy * 2 + cc, j)], abuf.at[block(slot), block(j)],
            a_send.at[i, j], a_recv.at[i, j], fs(xh, yy, cc),
        )

    def act_arrival(i, dy, dc, j):
        yy, cc = near(4 - dy, dc)
        place = abuf.at[block(yy * 2 + cc), block(j)]
        return remote(place, place, a_send.at[i, j], a_recv.at[i, j], mate)

    def part_send(u, h):
        rows = block(u)
        return remote(
            xsend.at[rows, quarter(h)], xrecv.at[rows, quarter(h)], x_send.at[u, h], x_recv.at[u, h], over
        )

    def pos_send(d, source):
        return remote(
            pos, pall.at[block(source, 32)], p_send.at[d - 1], p_recv.at[d - 1], rep(d)
        )

    def val_send(d, j, source):
        place = vall.at[source, block(j, 8)]
        return remote(place, place, v_send.at[d - 1, j], v_recv.at[d - 1, j], rep(d))

    def send_acts(j, carry=0):
        for i, (dy, dc) in enumerate(NEAR):
            act_send(i, dy, dc, j).start()
        return carry

    for h in range(4):
        for i, (dy, dc) in with_mate:
            cot_send(i, dy, dc, h).start()
        if h == 3:
            send_acts(4)
        send_acts(h)
        if h == 0:
            for d in range(1, 16):
                pos_send(d, r).start()
    lax.fori_loop(5, 8, send_acts, 0)
    get_mom.start()

    own_pos.wait()
    mine = pall[block(r, 32), :]
    turned[...] = jnp.concatenate([mine] * 4, 0).T
    lane_group = lax.broadcasted_iota(jnp.int32, (32, 128), 1) // 32
    rows32 = turned[pl.ds(0, 32, stride=4), :]
    for q in range(1, 4):
        rows32 = jnp.where(lane_group == q, turned[pl.ds(q, 32, stride=4), :], rows32)
    orow[...] = rows32
    lane1 = lax.broadcasted_iota(jnp.int32, (1, 128), 1) // 32 * 64
    iota256 = lax.broadcasted_iota(jnp.int32, (256, 128), 0)
    iota64 = lax.broadcasted_iota(jnp.int32, (64, 128), 0)

    def own_masks(p, carry):
        for q in range(4):
            t = p * 4 + q
            row = orow[pl.ds(t, 1), :]
            spread = one_hot(iota256, (row & 63) + lane1)
            wide[t] = spread
            kept[block(p, 64), q * 256 : q * 256 + 256] = dot_t(one_hot(iota64, row >> 6), spread).astype(BF)
        return carry

    def gather_rows():
        for d in range(1, 16):
            pos_send(d, (r + 16 - d) % 16).wait_recv()
        for k in range(4):
            prow[:, k * 128 : k * 128 + 128] = pall[k * 128 : k * 128 + 128, :].T

    iota512 = lax.broadcasted_iota(jnp.int32, (64, 512), 0).astype(jnp.int16)

    def all_masks(first):
        def group(g, carry):
            row = prow[pl.ds(g, 1), :]
            for part, out in ((row & 63, low_hot), (row >> 6, high_hot)):
                part = jnp.broadcast_to(part.astype(jnp.int16), (64, 512))
                out[g] = jnp.where(iota512 == part, jnp.ones((), BF), jnp.zeros((), BF))
            return carry

        lax.fori_loop(first, first + 64, group, 0)

    def wait_acts(j):
        for i, (dy, dc) in enumerate(NEAR):
            act_arrival(i, dy, dc, j).wait_recv()

    for h in range(4):
        for i, (dy, dc) in with_mate[1:3] + with_mate[:1] + with_mate[3:]:
            cot_arrival(i, dy, dc, h).wait_recv()
            if i < 3:
                cot_forward(i, h, c).start()
        for i in range(3):
            cot_forward(i, h, 1 - c).wait_recv()
        if h == 0:
            own_cot.wait()
            own_act[0].wait()
        else:
            done = 128 * h
            xsend[0:done, quarter(h)] = t_dot(abuf[:, 0:done], cbuf[:, quarter(h)]).astype(BF)
            for u in range(h):
                part_send(u, h).start()
        wait_acts(h)
        upto = 256 * (h + 1)
        xsend[block(h), 0:upto] = t_dot(abuf[:, block(h)], cbuf[:, 0:upto]).astype(BF)
        for k in range(h + 1):
            part_send(h, k).start()
        if h == 0:
            fill_tables(rt, lt)
            lax.fori_loop(0, 8, own_masks, 0)
        elif h == 1:
            gather_rows()
            all_masks(0)
        elif h == 2:
            all_masks(64)

    get_mom.wait()
    own_act[1].wait()

    def momentum(j):
        rows = block(j)
        wait_acts(j + 4)
        grad = t_dot(abuf[:, block(j + 4)], cbuf[...])
        for h in range(4):
            part_send(j, h).wait_recv()
        nm[rows, :] = 0.999 * mbuf[rows, :] + (grad + xrecv[rows, :].astype(F32))
        coeffs = transform(nm, rows, rt.at[0], lt.at[0])
        for q in range(4):
            cols = pl.ds(q * 256, 256)
            dense[:, cols] = coeffs[q] * kept[rows, cols].astype(F32)
            for p in range(2):
                t = j * 8 + p * 4 + q
                hi, lo = split(coeffs[q][p * 64 : p * 64 + 64])
                both = dot(jnp.concatenate([hi, lo], 0), wide[t])
                high = iota64 == (orow[pl.ds(t, 1), :] >> 6)
                picked = jnp.where(high, both[:64] + both[64:], 0.0)
                vall[r, pl.ds(t, 1), :] = jnp.sum(picked, axis=0, keepdims=True)
        for d in FAR_FIRST:
            val_send(d, j, r).start()
        for q, own in enumerate(transform(dense, pl.ds(0, 128), rt.at[1], lt.at[1])):
            cols = pl.ds(q * 256, 256)
            nm[rows, cols] = nm[rows, cols] - own

    lane8 = lax.broadcasted_iota(jnp.int32, (8, 128), 1) // 32

    def update(j):
        for d in range(1, 16):
            val_send(d, j, (r + 16 - d) % 16).wait_recv()
        for k in range(4):
            tiles = [vall[4 * k + b, block(j, 8), :] for b in range(4)]
            for q in range(4):
                merged = None
                for b in range(4):
                    shift = (b - q) * 32 % 128
                    moved = pltpu.roll(tiles[b], shift, 1) if shift else tiles[b]
                    merged = moved if b == 0 else jnp.where(lane8 == b, moved, merged)
                vrow[q, :, k * 128 : k * 128 + 128] = merged
        for t in range(8):
            parts = []
            for q in range(4):
                g = (j * 8 + t) * 4 + q
                val = vrow[q, t : t + 1, :]
                hi = val.astype(BF)
                lo = (val - hi.astype(F32)).astype(BF)
                hot = high_hot[g]
                both = dot_t(jnp.concatenate([hot * hi, hot * lo], 0), low_hot[g])
                parts.append(both[:64] + both[64:])
            row, col = t // 4 * 64, t % 4 * 256
            dense[row : row + 64, col : col + 256] = jnp.concatenate(parts, 1)
        for q, out in enumerate(transform(dense, pl.ds(0, 128), rt.at[1], lt.at[1])):
            st[block(j), q * 256 : q * 256 + 256] = jnp.tanh(4.0 * out)

    def all_sent():
        for h in range(4):
            for i, (dy, dc) in with_mate:
                cot_send(i, dy, dc, h).wait_send()
            for i in range(3):
                cot_forward(i, h, c).wait_send()
        for d in range(1, 16):
            pos_send(d, r).wait_send()

        def sent(j, carry):
            for i, (dy, dc) in enumerate(NEAR):
                act_send(i, dy, dc, j).wait_send()
                act_send(i, dy, dc, j + 4).wait_send()
            for h in range(4):
                part_send(j, h).wait_send()
            return carry

        lax.fori_loop(0, 4, sent, 0)

        def values_sent(j, carry):
            for d in range(1, 16):
                val_send(d, j, r).wait_send()
            return carry

        lax.fori_loop(0, 3, values_sent, 0)

    def stage(j, carry):
        @pl.when(j < 4)
        def _():
            momentum(j)

        @pl.when(j >= LAG)
        def _():
            update(j - LAG)

        @pl.when(j == 4)
        def _():
            all_sent()

        return carry

    lax.fori_loop(0, 4 + LAG, stage, 0)

    for d in range(1, 16):
        val_send(d, 3, r).wait_send()


def store_kernel(a, b, a_out, b_out, sems):
    copies = [
        pltpu.make_async_copy(src.at[pl.ds(k * 128, 128)], dst.at[pl.ds(k * 128, 128)], sems.at[i, k])
        for i, (src, dst) in enumerate(((a, a_out), (b, b_out)))
        for k in range(4)
    ]
    for copy in copies:
        copy.start()
    for copy in copies:
        copy.wait()


def per_device(activations, cotangent, momentum, positions):
    vmem = pl.BlockSpec(memory_space=pltpu.VMEM)
    hbm = pl.BlockSpec(memory_space=pltpu.HBM)
    dma = pltpu.SemaphoreType.DMA
    rows = jax.ShapeDtypeStruct((512, 1024), F32)
    nm, st = pl.pallas_call(
        step_kernel,
        out_shape=(rows, rows),
        in_specs=[hbm] * 4,
        out_specs=(vmem, vmem),
        scratch_shapes=[
            pltpu.VMEM((1024, 1024), BF),
            pltpu.VMEM((1024, 1024), BF),
            pltpu.VMEM((512, 1024), BF),
            pltpu.VMEM((512, 1024), BF),
            pltpu.VMEM((512, 1024), F32),
            pltpu.VMEM((512, 128), jnp.int32),
            pltpu.VMEM((16, 32, 128), F32),
            pltpu.VMEM((128, 512), jnp.int32),
            pltpu.VMEM((128, 128), jnp.int32),
            pltpu.VMEM((32, 128), jnp.int32),
            pltpu.VMEM((32, 256, 128), BF),
            pltpu.VMEM((512, 1024), BF),
            pltpu.VMEM((128, 64, 512), BF),
            pltpu.VMEM((128, 64, 512), BF),
            pltpu.VMEM((4, 8, 512), F32),
            pltpu.VMEM((128, 1024), F32),
            pltpu.VMEM((2, 512, 256), BF),
            pltpu.VMEM((2, 128, 384), BF),
            dma((4, 4)), dma((4, 4)), dma((3, 4)), dma((3, 4)), dma((7, 8)), dma((7, 8)), dma((4, 4)), dma((4, 4)),
            dma((15,)), dma((15,)), dma((15, 4)), dma((15, 4)), dma((5,)),
        ],
        name="step",
        compiler_params=pltpu.CompilerParams(
            collective_id=0, has_side_effects=True, vmem_limit_bytes=48 << 20
        ),
    )(activations[0], cotangent[0], momentum[0], positions[0].T)
    nm, st = pl.pallas_call(
        store_kernel,
        out_shape=(rows, rows),
        in_specs=[vmem, vmem],
        out_specs=(hbm, hbm),
        scratch_shapes=[dma((2, 4))],
        name="store",
        compiler_params=pltpu.CompilerParams(vmem_limit_bytes=1 << 20),
    )(nm, st)
    return nm[None], st


def solution(mesh):
    return jax.shard_map(
        per_device,
        mesh=mesh,
        in_specs=(
            P("rep", "fsdp", None),
            P("rep", "fsdp", None),
            P("rep", "fsdp", None),
            P("rep", "fsdp", None),
        ),
        out_specs=(P("rep", "fsdp", None), P("fsdp", None)),
        check_vma=False,
    )
```
